512 devices in a mesh: ops: 64 (over x, z_lo, y), wf: 8 (over z_hi, core).
Axes of the slice: x: 4, y: 8, z: 8 (z_hi: 4, z_lo: 2; z = z_hi * 2 + z_lo), core: 2. Of those that a mesh axis runs over, the one named last changes fastest.
Arguments:
- psi_one: float32 [16, 512, 512], P('wf', 'ops'), may hold values from -6 to 6
- psi_two: float32 [16, 512, 512], P('wf', 'ops'), may hold values from -6 to 6
- left_ops: float32 [64, 16, 512, 512], P('ops', 'wf'), may hold values from -0.03125 to 0.03125
- right_ops: float32 [64, 16, 512, 512], P('ops', 'wf'), may hold values from -0.25 to 0.25
- shift_ops: float32 [16, 512, 512], P('wf'), may hold values from -0.25 to 0.25
- block_dims: int32 [16], replicated, may hold values from 64 to 512, as said below
- partner: int32 [16], replicated, may hold values from 0 to 15, each once
Outputs:
- sigma_one: float32 [16, 512, 512], P('wf', 'ops')
- sigma_two: float32 [16, 512, 512], P('wf', 'ops')
The draws below stay inside these ranges and needn't reach their ends.
Inputs may be any that keep to these rules, and one draw needn't show every extreme that they name: `block_dims`: every block's live size; the largest block is 512 in every draw.
All inputs are finite; a program needn't handle non-finite values.
Results may differ from the reference program's by a relative error of at most 0.0001.
Values sent between devices are 32-bit elements; how exact they have to be, the bound alone decides.
No kernel may reach another device: no remote copies, remote signals or barrier semaphores. Data moves between devices by JAX's collectives and lax.ppermute only.
A program may use at most 64 MiB of HBM per device.

```python
import jax
import jax.numpy as jnp
from jax import lax

P_SIZE = 512
TERMS = 64
NB = 16


def draw_block_dims(key, part):
    key = jax.random.fold_in(key, 11)
    first, second = jax.random.split(key)
    sizes = jax.random.randint(first, (NB,), P_SIZE // 8, P_SIZE + 1)
    where = jax.random.randint(second, (), 0, NB)
    return jnp.where(jnp.arange(NB) == where, P_SIZE, sizes).astype(jnp.int32)


def block_levels(own_key, shape, pieces, smallest, top_value):
    loudness, own = 1.0, jax.random.fold_in(own_key, 6)
    for position, shards_of in pieces:
        steps = jnp.exp(jax.random.uniform(jax.random.fold_in(own, position), (shards_of,), jnp.float32, smallest / len(pieces), top_value / len(pieces)))
        loudness = loudness * jnp.repeat(steps, shape[position] // shards_of).reshape([-1 if axis == position else 1 for axis in range(len(shape))])
    return loudness


def bell_draw(key, shape, width, bound, shards=(), kind=jnp.bfloat16):
    array = width * jax.random.normal(key, shape, jnp.float32)
    if shards:
        array = array * block_levels(key, shape, shards, -0.22, 0.18)
    return jnp.clip(array, -bound, bound).astype(kind)


def setup_inputs(seed: int = 0) -> dict:
    key_of = jax.random.split(jax.random.key(seed), 8)
    return {
        "psi_one": bell_draw(key_of[0], (NB, P_SIZE, P_SIZE), 1.0, 6.0, ((0, 8), (1, 64)), jnp.float32),
        "psi_two": bell_draw(key_of[1], (NB, P_SIZE, P_SIZE), 1.0, 6.0, ((0, 8), (1, 64)), jnp.float32),
        "left_ops": bell_draw(key_of[2], (TERMS, NB, P_SIZE, P_SIZE), (P_SIZE * TERMS) ** -0.5, 0.03125, ((0, 64), (1, 8)), jnp.float32),
        "right_ops": bell_draw(key_of[3], (TERMS, NB, P_SIZE, P_SIZE), P_SIZE ** -0.5, 0.25, ((0, 64), (1, 8)), jnp.float32),
        "shift_ops": bell_draw(key_of[4], (NB, P_SIZE, P_SIZE), P_SIZE ** -0.5, 0.25, ((0, 8),), jnp.float32),
        "block_dims": draw_block_dims(jax.random.fold_in(key_of[7], 71), 0),
        "partner": jax.random.permutation(key_of[6], NB).astype(jnp.int32),
    }


def reference(psi_one, psi_two, left_ops, right_ops, shift_ops, block_dims, partner):
    highest = lax.Precision.HIGHEST
    index = jnp.arange(P_SIZE, dtype=jnp.int32)
    live_rows = (index[None, :] < block_dims[:, None]).astype(jnp.float32)
    mask = live_rows[:, :, None] * live_rows[:, None, :]

    def sigma_of(psi):
        live = psi * mask

        def per_block(block):
            current = live[block]

            def add_term(total, term):
                middle = jnp.dot(left_ops[term, block], current, precision=highest)
                return total + jnp.dot(middle, right_ops[term, block].T, precision=highest), None

            total, unused = lax.scan(add_term, jnp.zeros((P_SIZE, P_SIZE), jnp.float32), jnp.arange(TERMS, dtype=jnp.int32))
            other = live[partner[block]]
            total = total + jnp.dot(other, shift_ops[block].T, precision=highest)
            return total * mask[block]

        return lax.map(per_block, jnp.arange(NB, dtype=jnp.int32))

    return sigma_of(psi_one), sigma_of(psi_two)
```

```python
import jax
import jax.numpy as jnp
from jax import lax
from jax.sharding import Mesh, PartitionSpec as P

AXES = ("x", "zl", "yh", "yl", "zh", "c")
SIZES = (4, 2, 4, 2, 4, 2)
OPS = ("x", "zl", "yh", "yl")
WF = ("zh", "c")
FAR = ("zl", "yh")
NEAR = ("x", "yl")


def swap_pair(array):
    return lax.ppermute(array, "zl", [(0, 1), (1, 0)])


def per_device(psi_one, psi_two, left_ops, right_ops, shift_ops, block_dims, partner):
    high = lax.Precision.HIGH
    blocks, rows, width = psi_one.shape
    ops_index = lax.axis_index(OPS)
    wf_index = lax.axis_index(WF)
    mine = lax.axis_index("zl")

    local_dims = lax.dynamic_slice_in_dim(block_dims, wf_index * blocks, blocks)
    local_pairs = lax.dynamic_slice_in_dim(partner, wf_index * blocks, blocks)
    columns = jnp.arange(width, dtype=jnp.int32)
    row_ids = ops_index * rows + jnp.arange(rows, dtype=jnp.int32)
    col_live = columns[None, :] < local_dims[:, None]
    row_live = row_ids[None, :] < local_dims[:, None]
    mask = (row_live[:, :, None] & col_live[:, None, :]).astype(jnp.float32)
    live = jnp.stack([psi_one * mask, psi_two * mask], axis=1)

    other = 1 - mine
    left_in = swap_pair(lax.dynamic_index_in_dim(left_ops[0], other, 0, keepdims=False))
    right_in = swap_pair(lax.dynamic_index_in_dim(right_ops[0], other, 0, keepdims=False))
    left_own = lax.dynamic_index_in_dim(left_ops[0], mine, 0, keepdims=False)
    right_own = lax.dynamic_index_in_dim(right_ops[0], mine, 0, keepdims=False)

    far_out = jnp.broadcast_to(live[:, None], (2, 4, 2, rows, width)).reshape(8, 2, rows, width)
    far_in = lax.all_to_all(far_out, FAR, 0, 0, tiled=True)
    near_out = jnp.broadcast_to(far_in[None], (8,) + far_in.shape)
    near_in = lax.all_to_all(near_out, NEAR, 0, 0, tiled=True)

    full = near_in.reshape(4, 2, 2, 4, 2, rows, width)
    full = full.transpose(4, 0, 2, 3, 1, 5, 6).reshape(2, 64 * rows, width)

    total = 0.0
    for left, right in ((left_own, right_own), (left_in, right_in)):
        middle = jnp.einsum("ik,vkj->vij", left, full, precision=high)
        total = total + jnp.einsum("vij,lj->vil", middle, right, precision=high)

    near_back = total.reshape(2, 4, 2, 4, 2, rows, width).transpose(1, 4, 2, 3, 0, 5, 6)
    near_back = lax.all_to_all(near_back.reshape(8, 8, 2, rows, width), NEAR, 0, 0, tiled=True)
    near_sum = jnp.sum(near_back, axis=0)
    far_back = lax.all_to_all(near_sum, FAR, 0, 0, tiled=True)
    summed = jnp.sum(far_back.reshape(2, 4, 2, rows, width), axis=1)

    tied, unused = lax.optimization_barrier((live, near_in))
    every = lax.all_gather(tied, WF, axis=0, tiled=True)
    paired = jnp.take(every, local_pairs, axis=0, mode="clip")
    shifted = jnp.einsum("bvrp,bqp->bvrq", paired, shift_ops, precision=high)

    sigma = (summed + shifted) * mask[:, None]
    return sigma[:, 0], sigma[:, 1]


def solution(mesh):
    fine = Mesh(mesh.devices.reshape(SIZES), AXES)
    in_specs = (
        P(WF, OPS, None),
        P(WF, OPS, None),
        P(OPS, WF, None, None),
        P(OPS, WF, None, None),
        P(WF, None, None),
        P(),
        P(),
    )
    out_specs = (P(WF, OPS, None), P(WF, OPS, None))
    return jax.shard_map(
        per_device, mesh=fine, in_specs=in_specs, out_specs=out_specs, check_vma=False
    )
```

```python
import jax
import jax.numpy as jnp
from jax import lax
from jax.experimental import pallas as pl
from jax.experimental.pallas import tpu as pltpu
from jax.sharding import Mesh, PartitionSpec as P

AXES = ("x", "zl", "yh", "yl", "zh", "c")
SIZES = (4, 2, 4, 2, 4, 2)
OPS = ("x", "zl", "yh", "yl")
WF = ("zh", "c")
FAR = ("zl", "yh")
NEAR = ("x", "yl")
F32 = jnp.float32
BF16 = jnp.bfloat16
VMEM = pl.BlockSpec(memory_space=pltpu.VMEM)
SMEM = pl.BlockSpec(memory_space=pltpu.SMEM)
PARAMS = pltpu.CompilerParams(vmem_limit_bytes=48 * 1024 * 1024)


def shape(*dims):
    return jax.ShapeDtypeStruct(dims, F32)


def halves(value):
    high = value.astype(BF16)
    return high, (value - high.astype(F32)).astype(BF16)


def times(a, b):
    return jnp.dot(a, b, preferred_element_type=F32)


def times_t(a, b):
    return lax.dot_general(a, b, (((1,), (1,)), ((), ())), preferred_element_type=F32)


def live_mask(place_ref, dims_ref, block, rows, width):
    size = dims_ref[place_ref[1] * 2 + block]
    row = place_ref[0] * rows + lax.broadcasted_iota(jnp.int32, (rows, width), 0)
    column = lax.broadcasted_iota(jnp.int32, (rows, width), 1)
    return (row < size) & (column < size)


def swap(value):
    return lax.ppermute(value, "zl", [(0, 1), (1, 0)])


def after(value, earlier):
    return lax.optimization_barrier((value, earlier))[0]


def spread_kernel(place_ref, dims_ref, one_ref, two_ref, keep_ref, send_ref, live_ref):
    blocks, rows, width = one_ref.shape
    mine = place_ref[0] // 8 % 2
    for ref, block in ((keep_ref, mine), (send_ref, 1 - mine)):
        mask = live_mask(place_ref, dims_ref, block, rows, width)
        for vector, psi_ref in enumerate((one_ref, two_ref)):
            live = jnp.where(mask, psi_ref[block], 0.0)
            ref[vector] = live
            live_ref[block, vector] = live


def product_kernel(
    mine_ref, g_ref, l_ref, r_ref, l_in_ref, r_in_ref, out_ref, ph, pw, mh, ml, rh, rl
):
    width = g_ref.shape[-1]
    half = width // 2
    for x in range(4):
        for z in range(2):
            part = g_ref[x, :, :, (z + mine_ref[0]) % 2, 0].transpose(1, 0, 2, 3).reshape(64, width)
            rows = pl.ds(x * 128 + z * 64, 64)
            ph[rows], pw[rows] = halves(part)
    for t, (left, right) in enumerate(
        ((l_ref.at[0, 0], r_ref.at[0, 0]), (l_in_ref, r_in_ref))
    ):
        for i in range(2):
            rows = pl.ds(i * half, half)
            high, low = halves(left[rows])
            m = times(high, ph[...]) + times(low, ph[...]) + times(high, pw[...])
            mh[t, rows], ml[t, rows] = halves(m)
            rh[t, rows], rl[t, rows] = halves(right[rows])
    for i in range(2):
        rows = pl.ds(i * half, half)
        s = times_t(mh[0, rows], rh[0]) + times_t(ml[0, rows], rh[0]) + times_t(mh[0, rows], rl[0])
        s += times_t(mh[1, rows], rh[1]) + times_t(ml[1, rows], rh[1]) + times_t(mh[1, rows], rl[1])
        s = s.reshape(2, 2, 4, 2, 8, width).transpose(0, 3, 1, 2, 4, 5)
        out_ref[pl.ds(i * 2, 2)] = s


def sum_kernel(one_ref, two_ref, out_ref):
    for vector, ref in enumerate((one_ref, two_ref)):
        total = ref[0]
        for source in range(1, ref.shape[0]):
            total = total + ref[source]
        out_ref[:, vector] = total


def shift_kernel(place_ref, pair_ref, *refs):
    every, (shift_ref, out_ref) = refs[:4], refs[4:]
    blocks, width = shift_ref.shape[0], shift_ref.shape[-1]
    for block in range(blocks):
        pair = pair_ref[place_ref[1] * 2 + block]
        owner = pair // 2
        step = (owner // 2 - place_ref[1] // 2 + 4) % 4
        core = (owner + place_ref[1]) % 2
        paired = every[0][core, pair % 2]
        for other in range(1, 4):
            paired = jnp.where(step == other, every[other][core, pair % 2], paired)
        high, low = halves(paired.reshape(16, width))
        s_high, s_low = halves(shift_ref[block])
        out = times_t(high, s_high) + times_t(low, s_high) + times_t(high, s_low)
        out_ref[block] = out.reshape(2, 8, width)


def final_kernel(place_ref, dims_ref, back_ref, shifted_ref, one_ref, two_ref):
    blocks, rows, width = one_ref.shape
    for block in range(blocks):
        mask = live_mask(place_ref, dims_ref, block, rows, width)
        for vector, ref in enumerate((one_ref, two_ref)):
            total = shifted_ref[block, vector]
            for source in range(4):
                total = total + back_ref[block * 4 + source, vector]
            ref[block] = jnp.where(mask, total, 0.0)


def per_device(psi_one, psi_two, left_ops, right_ops, shift_ops, block_dims, partner):
    blocks, rows, width = psi_one.shape
    place = jnp.stack([lax.axis_index(OPS), lax.axis_index(WF)]).astype(jnp.int32)

    keep, send, live = pl.pallas_call(
        spread_kernel,
        out_shape=(shape(2, rows, width), shape(2, rows, width), shape(2, 2, rows, width)),
        in_specs=[SMEM, SMEM, VMEM, VMEM],
        out_specs=(VMEM, VMEM, VMEM),
        compiler_params=PARAMS,
        name="spread",
    )(place, block_dims, psi_one, psi_two)

    mine = lax.axis_index("zl").astype(jnp.int32)
    got = swap(send)
    left_out = lax.dynamic_index_in_dim(left_ops[0], 1 - mine, 0, keepdims=False)
    right_out = lax.dynamic_index_in_dim(right_ops[0], 1 - mine, 0, keepdims=False)
    got, left_out, right_out = lax.optimization_barrier((got, left_out, right_out))
    left_in = swap(left_out)
    right_in = swap(right_out)
    mine = mine[None]

    far_out = jnp.broadcast_to(jnp.stack([keep, got])[None], (4, 2, 2, rows, width))
    far_in = lax.all_to_all(far_out, "yh", 0, 0, tiled=True)

    other_core = lax.ppermute(live, "c", [(0, 1), (1, 0)])
    far_in, other_core = lax.optimization_barrier((far_in, other_core))

    near_out = jnp.broadcast_to(far_in[None], (8, 4, 2, 2, rows, width))
    near_in = lax.cond(
        lax.optimization_barrier(jnp.bool_(True)),
        lambda value: lax.all_to_all(value, NEAR, 0, 0, tiled=True),
        lambda value: value,
        near_out,
    )
    near_in, left_in, right_in = lax.optimization_barrier((near_in, left_in, right_in))

    near_backs = []
    for vector in range(2):
        sums = pl.pallas_call(
            product_kernel,
            out_shape=shape(4, 2, 2, 4, rows, width),
            grid_spec=pltpu.PrefetchScalarGridSpec(
                num_scalar_prefetch=1,
                grid=(1,),
                in_specs=[
                    pl.BlockSpec(
                        (4, 2, 4, 2, 1, rows, width),
                        lambda i, mine, vector=vector: (0, 0, 0, 0, vector, 0, 0),
                    ),
                    pl.BlockSpec((1, 1, width, width), lambda i, mine: (0, mine[0], 0, 0)),
                    pl.BlockSpec((1, 1, width, width), lambda i, mine: (0, mine[0], 0, 0)),
                    pl.BlockSpec((width, width), lambda i, mine: (0, 0)),
                    pl.BlockSpec((width, width), lambda i, mine: (0, 0)),
                ],
                out_specs=pl.BlockSpec(
                    (4, 2, 2, 4, rows, width), lambda i, mine: (0, 0, 0, 0, 0, 0)
                ),
                scratch_shapes=[
                    pltpu.VMEM((width, width), BF16),
                    pltpu.VMEM((width, width), BF16),
                    pltpu.VMEM((2, width, width), BF16),
                    pltpu.VMEM((2, width, width), BF16),
                    pltpu.VMEM((2, width, width), BF16),
                    pltpu.VMEM((2, width, width), BF16),
                ],
            ),
            compiler_params=PARAMS,
            cost_estimate=pl.CostEstimate(
                flops=12 * 2 * 512**3, bytes_accessed=8 * 2**20, transcendentals=0
            ),
            name="products",
        )(
            mine,
            near_in.reshape(4, 2, 4, 2, 2, rows, width),
            left_ops,
            right_ops,
            left_in,
            right_in,
        )

        near_backs.append(
            lax.all_to_all(sums.reshape(8, 8, rows, width), NEAR, 0, 0, tiled=True)
        )

    chip = after(jnp.stack([live, other_core]), near_in)
    every = [chip] + [
        lax.ppermute(chip, "zh", [((i + step) % 4, i) for i in range(4)]) for step in (1, 2, 3)
    ]

    near_sum = pl.pallas_call(
        sum_kernel,
        out_shape=shape(8, 2, rows, width),
        in_specs=[VMEM, VMEM],
        out_specs=VMEM,
        compiler_params=PARAMS,
        name="near_sum",
    )(*near_backs)
    near_sum, every[1], every[2] = lax.optimization_barrier((near_sum, every[1], every[2]))
    far_back = lax.all_to_all(near_sum, FAR, 0, 0, tiled=True)

    shifted = pl.pallas_call(
        shift_kernel,
        out_shape=shape(blocks, 2, rows, width),
        in_specs=[SMEM, SMEM, VMEM, VMEM, VMEM, VMEM, VMEM],
        out_specs=VMEM,
        compiler_params=PARAMS,
        cost_estimate=pl.CostEstimate(
            flops=3 * 2 * 32 * 512**2, bytes_accessed=3 * 2**20, transcendentals=0
        ),
        name="shift",
    )(place, partner, *every, shift_ops)

    return pl.pallas_call(
        final_kernel,
        out_shape=(shape(blocks, rows, width), shape(blocks, rows, width)),
        in_specs=[SMEM, SMEM, VMEM, VMEM],
        out_specs=(VMEM, VMEM),
        compiler_params=PARAMS,
        name="finish",
    )(place, block_dims, far_back, shifted)


def solution(mesh):
    fine = Mesh(mesh.devices.reshape(SIZES), AXES)
    in_specs = (
        P(WF, OPS, None),
        P(WF, OPS, None),
        P(OPS, WF, None, None),
        P(OPS, WF, None, None),
        P(WF, None, None),
        P(),
        P(),
    )
    out_specs = (P(WF, OPS, None), P(WF, OPS, None))
    return jax.shard_map(
        per_device, mesh=fine, in_specs=in_specs, out_specs=out_specs, check_vma=False
    )
```

```python
import functools

import jax
import jax.numpy as jnp
from jax import lax
from jax.experimental import pallas as pl
from jax.experimental.pallas import tpu as pltpu
from jax.sharding import Mesh, PartitionSpec as P

AXES = ("x", "zl", "yh", "yl", "zh", "c")
SIZES = (4, 2, 4, 2, 4, 2)
OPS = ("x", "zl", "yh", "yl")
WF = ("zh", "c")
FAR = ("zl", "yh")
NEAR = ("x", "yl")
F32 = jnp.float32
BF16 = jnp.bfloat16
VMEM = pl.BlockSpec(memory_space=pltpu.VMEM)
SMEM = pl.BlockSpec(memory_space=pltpu.SMEM)
HBM = pl.BlockSpec(memory_space=pl.ANY)
PARAMS = pltpu.CompilerParams(vmem_limit_bytes=48 * 1024 * 1024)
WIDE = pltpu.CompilerParams(vmem_limit_bytes=60 * 1024 * 1024)


def shape(*dims):
    return jax.ShapeDtypeStruct(dims, F32)


def halves(value):
    high = value.astype(BF16)
    return high, (value - high.astype(F32)).astype(BF16)


def times(a, b):
    return jnp.dot(a, b, preferred_element_type=F32)


def times_t(a, b):
    return lax.dot_general(a, b, (((1,), (1,)), ((), ())), preferred_element_type=F32)


def live_mask(place, place_ref, dims_ref, block, rows, width):
    size = dims_ref[place_ref[1] * 2 + block]
    row = place * rows + lax.broadcasted_iota(jnp.int32, (rows, width), 0)
    column = lax.broadcasted_iota(jnp.int32, (rows, width), 1)
    return (row < size) & (column < size)


def swap(value):
    return lax.ppermute(value, "zl", [(0, 1), (1, 0)])


def after(value, earlier):
    return lax.optimization_barrier((value, earlier))[0]


def pick_kernel(spot_ref, left_ref, right_ref, out_ref, held, in_sems, out_sems):
    quarter = held.shape[1] // 4
    pieces = [(side, pl.ds(i * quarter, quarter)) for side in range(2) for i in range(4)]
    ins, outs = [], []
    for at, (side, rows) in enumerate(pieces):
        source = (left_ref, right_ref)[side].at[0, 1 - spot_ref[0], rows]
        ins.append(pltpu.make_async_copy(source, held.at[side, rows], in_sems.at[at]))
        outs.append(
            pltpu.make_async_copy(held.at[side, rows], out_ref.at[side, rows], out_sems.at[at])
        )
    for copy in ins:
        copy.start()
    for copy_in, copy_out in zip(ins, outs):
        copy_in.wait()
        copy_out.start()
    for copy in outs:
        copy.wait()


def spread_kernel(place_ref, dims_ref, one_ref, two_ref, got_ref, far_ref, live_ref):
    blocks, rows, width = one_ref.shape
    mine = place_ref[0] // 8 % 2
    for block in range(blocks):
        mask = live_mask(place_ref[0], place_ref, dims_ref, block, rows, width)
        for vector, ref in enumerate((one_ref, two_ref)):
            live_ref[block, vector] = jnp.where(mask, ref[block], 0.0)
    neighbour = place_ref[0] + 8 - 16 * mine
    mask = live_mask(neighbour, place_ref, dims_ref, mine, rows, width)
    for vector in range(2):
        own = live_ref[mine, vector]
        got = jnp.where(mask, got_ref[vector], 0.0)
        for slot in range(4):
            far_ref[slot, 0, vector] = own
            far_ref[slot, 1, vector] = got


def product_kernel(
    vector, spot_ref, g_ref, l_ref, r_ref, pair_ref, out_ref,
    g, ops, out, ph, pw, mh, ml, rh, rl, sems, out_sems,
):
    width = g.shape[-1]
    half = width // 2
    sources = (l_ref.at[0, spot_ref[0]], pair_ref.at[0], r_ref.at[0, spot_ref[0]], pair_ref.at[1])
    loads = [pltpu.make_async_copy(g_ref.at[:, :, :, :, vector], g, sems.at[4])] + [
        pltpu.make_async_copy(source, ops.at[at], sems.at[at]) for at, source in enumerate(sources)
    ]
    for load in loads:
        load.start()
    loads[0].wait()
    for x in range(4):
        for z in range(2):
            part = g[x, :, :, (z + spot_ref[0]) % 2].transpose(1, 0, 2, 3).reshape(64, width)
            rows = pl.ds(x * 128 + z * 64, 64)
            ph[rows], pw[rows] = halves(part)
    for t in range(2):
        loads[1 + t].wait()
        for i in range(2):
            rows = pl.ds(i * half, half)
            high, low = halves(ops[t, rows])
            m = times(high, ph[...]) + times(low, ph[...]) + times(high, pw[...])
            mh[t, rows], ml[t, rows] = halves(m)
    for t in range(2):
        loads[3 + t].wait()
        rh[t], rl[t] = halves(ops[2 + t])
    stores = []
    for i in range(2):
        rows = pl.ds(i * half, half)
        s = times_t(mh[0, rows], rh[0]) + times_t(ml[0, rows], rh[0]) + times_t(mh[0, rows], rl[0])
        s += times_t(mh[1, rows], rh[1]) + times_t(ml[1, rows], rh[1]) + times_t(mh[1, rows], rl[1])
        s = s.reshape(2, 2, 4, 2, 8, width).transpose(0, 3, 1, 2, 4, 5)
        out[pl.ds(i * 2, 2)] = s
        place = pl.ds(i * 2, 2)
        stores.append(pltpu.make_async_copy(out.at[place], out_ref.at[place], out_sems.at[i]))
        stores[-1].start()
    for store in stores:
        store.wait()


def sum_kernel(one_ref, two_ref, out_ref):
    for vector, ref in enumerate((one_ref, two_ref)):
        total = ref[0]
        for source in range(1, ref.shape[0]):
            total = total + ref[source]
        out_ref[:, vector] = total


def held_rows(place_ref, pair, chip_ref, next_ref):
    wf, core = place_ref[1], (pair // 2 + place_ref[1]) % 2
    here = (pair // 4 + wf // 2) % 2 == 0
    return jnp.where(here, chip_ref[core, pair % 2], next_ref[core, pair % 2])


def choose_kernel(place_ref, pair_ref, chip_ref, next_ref, out_ref):
    far_wf = (place_ref[1] + 4) % 8
    for block in range(out_ref.shape[0]):
        out_ref[block] = held_rows(place_ref, pair_ref[far_wf * 2 + block], chip_ref, next_ref)


def shift_kernel(place_ref, pair_ref, chip_ref, next_ref, far_ref, shift_ref, out_ref):
    blocks, width = shift_ref.shape[0], shift_ref.shape[-1]
    for block in range(blocks):
        pair = pair_ref[place_ref[1] * 2 + block]
        held = pair // 8 == place_ref[1] // 4
        paired = jnp.where(held, held_rows(place_ref, pair, chip_ref, next_ref), far_ref[block])
        high, low = halves(paired.reshape(16, width))
        s_high, s_low = halves(shift_ref[block])
        out = times_t(high, s_high) + times_t(low, s_high) + times_t(high, s_low)
        out_ref[block] = out.reshape(2, 8, width)


def final_kernel(place_ref, dims_ref, back_ref, shifted_ref, one_ref, two_ref):
    blocks, rows, width = one_ref.shape
    for block in range(blocks):
        mask = live_mask(place_ref[0], place_ref, dims_ref, block, rows, width)
        for vector, ref in enumerate((one_ref, two_ref)):
            total = shifted_ref[block, vector]
            for source in range(4):
                total = total + back_ref[block * 4 + source, vector]
            ref[block] = jnp.where(mask, total, 0.0)


def per_device(psi_one, psi_two, left_ops, right_ops, shift_ops, block_dims, partner):
    blocks, rows, width = psi_one.shape
    place = jnp.stack([lax.axis_index(OPS), lax.axis_index(WF)]).astype(jnp.int32)

    mine = lax.axis_index("zl").astype(jnp.int32)
    spot = mine[None]
    got = swap(
        jnp.stack(
            [lax.dynamic_index_in_dim(psi, 1 - mine, 0, False) for psi in (psi_one, psi_two)]
        )
    )
    pair_out = pl.pallas_call(
        pick_kernel,
        out_shape=shape(2, width, width),
        in_specs=[SMEM, HBM, HBM],
        out_specs=HBM,
        scratch_shapes=[
            pltpu.VMEM((2, width, width), F32),
            pltpu.SemaphoreType.DMA((8,)),
            pltpu.SemaphoreType.DMA((8,)),
        ],
        compiler_params=WIDE,
        name="pick",
    )(spot, left_ops, right_ops)
    got, pair_out = lax.optimization_barrier((got, pair_out))
    pair_in = swap(pair_out)

    far_out, live = pl.pallas_call(
        spread_kernel,
        out_shape=(shape(4, 2, 2, rows, width), shape(blocks, 2, rows, width)),
        in_specs=[SMEM, SMEM, VMEM, VMEM, VMEM],
        out_specs=(VMEM, VMEM),
        compiler_params=PARAMS,
        name="spread",
    )(place, block_dims, psi_one, psi_two, got)
    far_in = lax.all_to_all(far_out, "yh", 0, 0, tiled=True)

    other_core = lax.ppermute(live, "c", [(0, 1), (1, 0)])
    far_in, other_core = lax.optimization_barrier((far_in, other_core))

    near_in = lax.cond(
        lax.optimization_barrier(jnp.bool_(True)),
        lambda value: lax.all_to_all(
            jnp.broadcast_to(value[None], (8,) + value.shape), NEAR, 0, 0, tiled=True
        ),
        lambda value: jnp.zeros((8,) + value.shape, F32),
        far_in,
    )
    near_in, pair_in = lax.optimization_barrier((near_in, pair_in))

    products = []
    for vector in range(2):
        sums = pl.pallas_call(
            functools.partial(product_kernel, vector),
            out_shape=shape(4, 2, 2, 4, rows, width),
            in_specs=[SMEM, HBM, HBM, HBM, HBM],
            out_specs=HBM,
            scratch_shapes=[
                pltpu.VMEM((4, 2, 4, 2, rows, width), F32),
                pltpu.VMEM((4, width, width), F32),
                pltpu.VMEM((4, 2, 2, 4, rows, width), F32),
                pltpu.VMEM((width, width), BF16),
                pltpu.VMEM((width, width), BF16),
                pltpu.VMEM((2, width, width), BF16),
                pltpu.VMEM((2, width, width), BF16),
                pltpu.VMEM((2, width, width), BF16),
                pltpu.VMEM((2, width, width), BF16),
                pltpu.SemaphoreType.DMA((5,)),
                pltpu.SemaphoreType.DMA((2,)),
            ],
            compiler_params=WIDE,
            cost_estimate=pl.CostEstimate(
                flops=12 * 2 * 512**3, bytes_accessed=8 * 2**20, transcendentals=0
            ),
            name="products",
        )(spot, near_in.reshape(4, 2, 4, 2, 2, rows, width), left_ops, right_ops, pair_in)
        products.append(sums.reshape(8, 8, rows, width))

    chip = after(jnp.stack([live, other_core]), near_in)
    next_chip = lax.ppermute(chip, "zh", [(0, 1), (1, 0), (2, 3), (3, 2)])

    near_back_one = lax.all_to_all(products[0], NEAR, 0, 0, tiled=True)
    products[1], next_chip = lax.optimization_barrier((products[1], next_chip))
    near_backs = [near_back_one, lax.all_to_all(products[1], NEAR, 0, 0, tiled=True)]
    near_sum = pl.pallas_call(
        sum_kernel,
        out_shape=shape(8, 2, rows, width),
        in_specs=[VMEM, VMEM],
        out_specs=VMEM,
        compiler_params=PARAMS,
        name="near_sum",
    )(*near_backs)
    chosen = pl.pallas_call(
        choose_kernel,
        out_shape=shape(blocks, 2, rows, width),
        in_specs=[SMEM, SMEM, VMEM, VMEM],
        out_specs=VMEM,
        compiler_params=PARAMS,
        name="choose",
    )(place, partner, chip, next_chip)
    from_far = lax.ppermute(chosen, "zh", [(0, 2), (2, 0), (1, 3), (3, 1)])
    near_sum, from_far = lax.optimization_barrier((near_sum, from_far))
    far_back = lax.all_to_all(near_sum, FAR, 0, 0, tiled=True)

    shifted = pl.pallas_call(
        shift_kernel,
        out_shape=shape(blocks, 2, rows, width),
        in_specs=[SMEM, SMEM] + [VMEM] * 4,
        out_specs=VMEM,
        compiler_params=PARAMS,
        cost_estimate=pl.CostEstimate(
            flops=3 * 2 * 32 * 512**2, bytes_accessed=3 * 2**20, transcendentals=0
        ),
        name="shift",
    )(place, partner, chip, next_chip, from_far, shift_ops)

    return pl.pallas_call(
        final_kernel,
        out_shape=(shape(blocks, rows, width), shape(blocks, rows, width)),
        in_specs=[SMEM, SMEM, VMEM, VMEM],
        out_specs=(VMEM, VMEM),
        compiler_params=PARAMS,
        name="finish",
    )(place, block_dims, far_back, shifted)


def solution(mesh):
    fine = Mesh(mesh.devices.reshape(SIZES), AXES)
    in_specs = (
        P(WF, OPS, None),
        P(WF, OPS, None),
        P(OPS, WF, None, None),
        P(OPS, WF, None, None),
        P(WF, None, None),
        P(),
        P(),
    )
    out_specs = (P(WF, OPS, None), P(WF, OPS, None))
    return jax.shard_map(
        per_device, mesh=fine, in_specs=in_specs, out_specs=out_specs, check_vma=False
    )
```

```python
import functools

import jax
import jax.numpy as jnp
from jax import lax
from jax.experimental import pallas as pl
from jax.experimental.pallas import tpu as pltpu
from jax.sharding import Mesh, PartitionSpec as P

AXES = ("xh", "xl", "zl", "yh", "yl", "zh", "c")
SIZES = (2, 2, 2, 4, 2, 4, 2)
OPS = ("xh", "xl", "zl", "yh", "yl")
WF = ("zh", "c")
F32 = jnp.float32
BF16 = jnp.bfloat16
VMEM = pl.BlockSpec(memory_space=pltpu.VMEM)
SMEM = pl.BlockSpec(memory_space=pltpu.SMEM)
HBM = pl.BlockSpec(memory_space=pl.ANY)
PARAMS = pltpu.CompilerParams(vmem_limit_bytes=48 * 1024 * 1024)
WIDE = pltpu.CompilerParams(vmem_limit_bytes=60 * 1024 * 1024)


def shape(*dims):
    return jax.ShapeDtypeStruct(dims, F32)


def halves(value):
    high = value.astype(BF16)
    return high, (value - high.astype(F32)).astype(BF16)


def times(a, b):
    return jnp.dot(a, b, preferred_element_type=F32)


def times_t(a, b):
    return lax.dot_general(a, b, (((1,), (1,)), ((), ())), preferred_element_type=F32)


def live_mask(place, place_ref, dims_ref, block, rows, width):
    size = dims_ref[place_ref[1] * 2 + block]
    row = place * rows + lax.broadcasted_iota(jnp.int32, (rows, width), 0)
    column = lax.broadcasted_iota(jnp.int32, (rows, width), 1)
    return (row < size) & (column < size)


def swap(value):
    return lax.ppermute(value, "zl", [(0, 1), (1, 0)])


def after(value, earlier):
    return lax.optimization_barrier((value, earlier))[0]


def pick_kernel(spot_ref, left_ref, right_ref, out_ref, held, in_sems, out_sems):
    quarter = held.shape[1] // 4
    pieces = [(side, pl.ds(i * quarter, quarter)) for side in range(2) for i in range(4)]
    ins, outs = [], []
    for at, (side, rows) in enumerate(pieces):
        source = (left_ref, right_ref)[side].at[0, 1 - spot_ref[0], rows]
        ins.append(pltpu.make_async_copy(source, held.at[side, rows], in_sems.at[at]))
        outs.append(
            pltpu.make_async_copy(held.at[side, rows], out_ref.at[side, rows], out_sems.at[at])
        )
    for copy in ins:
        copy.start()
    for copy_in, copy_out in zip(ins, outs):
        copy_in.wait()
        copy_out.start()
    for copy in outs:
        copy.wait()


def spread_kernel(place_ref, dims_ref, one_ref, two_ref, got_ref, far_ref, live_ref):
    blocks, rows, width = one_ref.shape
    mine = place_ref[0] // 8 % 2
    for block in range(blocks):
        mask = live_mask(place_ref[0], place_ref, dims_ref, block, rows, width)
        for vector, ref in enumerate((one_ref, two_ref)):
            live_ref[block, vector] = jnp.where(mask, ref[block], 0.0)
    neighbour = place_ref[0] + 8 - 16 * mine
    mask = live_mask(neighbour, place_ref, dims_ref, mine, rows, width)
    for vector in range(2):
        own = live_ref[mine, vector]
        got = jnp.where(mask, got_ref[vector], 0.0)
        for slot in range(4):
            far_ref[slot, 0, vector] = own
            far_ref[slot, 1, vector] = got


def product_kernel(
    place_ref, g_ref, l_ref, r_ref, pair_ref, out_ref,
    g, ops, out, ph, pw, mh, ml, rh, rl, sems, out_sems,
):
    width = g.shape[-1]
    half = width // 2
    mine = place_ref[0] // 8 % 2
    sources = (l_ref.at[0, mine], pair_ref.at[0], r_ref.at[0, mine], pair_ref.at[1])
    loads = [pltpu.make_async_copy(g_ref, g, sems.at[4])] + [
        pltpu.make_async_copy(source, ops.at[at], sems.at[at]) for at, source in enumerate(sources)
    ]
    for load in loads:
        load.start()
    loads[0].wait()
    for v in range(2):
        for x in range(4):
            for z in range(2):
                part = g[x, :, :, (z + mine) % 2, v].transpose(1, 0, 2, 3).reshape(64, width)
                rows = pl.ds(x * 128 + z * 64, 64)
                ph[v, rows], pw[v, rows] = halves(part)
    for t in range(2):
        loads[1 + t].wait()
        for i in range(2):
            rows = pl.ds(i * half, half)
            high, low = halves(ops[t, rows])
            for v in range(2):
                m = times(high, ph[v]) + times(low, ph[v]) + times(high, pw[v])
                mh[v, t, rows], ml[v, t, rows] = halves(m)
    for t in range(2):
        loads[3 + t].wait()
        rh[t], rl[t] = halves(ops[2 + t])
    stores = []
    for v in range(2):
        for i in range(2):
            rows = pl.ds(i * half, half)
            s = jnp.zeros((half, width), F32)
            for t in range(2):
                s += times_t(mh[v, t, rows], rh[t]) + times_t(ml[v, t, rows], rh[t])
                s += times_t(mh[v, t, rows], rl[t])
            s = s.reshape(2, 2, 4, 2, 8, width)
            for xl in range(2):
                for yl in range(2):
                    out[i, xl, yl, :, :, v] = s[xl, :, :, yl]
            stores.append(
                pltpu.make_async_copy(
                    out.at[i, :, :, :, :, v], out_ref.at[i, :, :, :, :, v], out_sems.at[v * 2 + i]
                )
            )
            stores[-1].start()
    for store in stores:
        store.wait()


def sum_kernel(in_ref, out_ref):
    total = in_ref[0]
    for source in range(1, in_ref.shape[0]):
        total = total + in_ref[source]
    out_ref[...] = total


def held_rows(place_ref, pair, chip_ref, next_ref):
    wf, core = place_ref[1], (pair // 2 + place_ref[1]) % 2
    here = (pair // 4 + wf // 2) % 2 == 0
    return jnp.where(here, chip_ref[core, pair % 2], next_ref[core, pair % 2])


def choose_kernel(place_ref, pair_ref, chip_ref, next_ref, out_ref):
    far_wf = (place_ref[1] + 4) % 8
    for block in range(out_ref.shape[0]):
        out_ref[block] = held_rows(place_ref, pair_ref[far_wf * 2 + block], chip_ref, next_ref)


def shift_kernel(place_ref, pair_ref, chip_ref, next_ref, far_ref, shift_ref, out_ref):
    blocks, width = shift_ref.shape[0], shift_ref.shape[-1]
    for block in range(blocks):
        pair = pair_ref[place_ref[1] * 2 + block]
        held = pair // 8 == place_ref[1] // 4
        paired = jnp.where(held, held_rows(place_ref, pair, chip_ref, next_ref), far_ref[block])
        high, low = halves(paired.reshape(16, width))
        s_high, s_low = halves(shift_ref[block])
        out = times_t(high, s_high) + times_t(low, s_high) + times_t(high, s_low)
        out_ref[block] = out.reshape(2, 8, width)


def final_kernel(place_ref, dims_ref, back_ref, shifted_ref, one_ref, two_ref):
    blocks, rows, width = one_ref.shape
    for block in range(blocks):
        mask = live_mask(place_ref[0], place_ref, dims_ref, block, rows, width)
        for vector, ref in enumerate((one_ref, two_ref)):
            total = shifted_ref[block, vector]
            for source in range(4):
                total = total + back_ref[block * 4 + source, vector]
            ref[block] = jnp.where(mask, total, 0.0)


def per_device(psi_one, psi_two, left_ops, right_ops, shift_ops, block_dims, partner):
    blocks, rows, width = psi_one.shape
    place = jnp.stack([lax.axis_index(OPS), lax.axis_index(WF)]).astype(jnp.int32)

    mine = lax.axis_index("zl").astype(jnp.int32)
    spot = mine[None]
    got = swap(
        jnp.stack(
            [lax.dynamic_index_in_dim(psi, 1 - mine, 0, False) for psi in (psi_one, psi_two)]
        )
    )
    pair_out = pl.pallas_call(
        pick_kernel,
        out_shape=shape(2, width, width),
        in_specs=[SMEM, HBM, HBM],
        out_specs=HBM,
        scratch_shapes=[
            pltpu.VMEM((2, width, width), F32),
            pltpu.SemaphoreType.DMA((8,)),
            pltpu.SemaphoreType.DMA((8,)),
        ],
        compiler_params=WIDE,
        name="pick",
    )(spot, left_ops, right_ops)
    got, pair_out = lax.optimization_barrier((got, pair_out))
    pair_in = swap(pair_out)

    far_out, live = pl.pallas_call(
        spread_kernel,
        out_shape=(shape(4, 2, 2, rows, width), shape(blocks, 2, rows, width)),
        in_specs=[SMEM, SMEM, VMEM, VMEM, VMEM],
        out_specs=(VMEM, VMEM),
        compiler_params=PARAMS,
        name="spread",
    )(place, block_dims, psi_one, psi_two, got)
    far_in = lax.all_to_all(far_out, "yh", 0, 0, tiled=True)

    other_core = lax.ppermute(live, "c", [(0, 1), (1, 0)])
    far_in, other_core = lax.optimization_barrier((far_in, other_core))

    near_in = lax.cond(
        lax.optimization_barrier(jnp.bool_(True)),
        lambda value: lax.all_to_all(
            jnp.broadcast_to(value[None], (8,) + value.shape), ("xh", "xl", "yl"), 0, 0, tiled=True
        ),
        lambda value: jnp.zeros((8,) + value.shape, F32),
        far_in,
    )
    near_in, pair_in = lax.optimization_barrier((near_in, pair_in))

    products = pl.pallas_call(
        product_kernel,
        out_shape=shape(2, 2, 2, 2, 4, 2, rows, width),
        in_specs=[SMEM, HBM, HBM, HBM, HBM],
        out_specs=HBM,
        scratch_shapes=[
            pltpu.VMEM((4, 2, 4, 2, 2, rows, width), F32),
            pltpu.VMEM((4, width, width), F32),
            pltpu.VMEM((2, 2, 2, 2, 4, 2, rows, width), F32),
            pltpu.VMEM((2, width, width), BF16),
            pltpu.VMEM((2, width, width), BF16),
            pltpu.VMEM((2, 2, width, width), BF16),
            pltpu.VMEM((2, 2, width, width), BF16),
            pltpu.VMEM((2, width, width), BF16),
            pltpu.VMEM((2, width, width), BF16),
            pltpu.SemaphoreType.DMA((5,)),
            pltpu.SemaphoreType.DMA((4,)),
        ],
        compiler_params=WIDE,
        cost_estimate=pl.CostEstimate(
            flops=24 * 2 * 512**3, bytes_accessed=8 * 2**20, transcendentals=0
        ),
        name="products",
    )(place, near_in.reshape(4, 2, 4, 2, 2, rows, width), left_ops, right_ops, pair_in)

    chip = after(jnp.stack([live, other_core]), near_in)
    next_chip = lax.ppermute(chip, "zh", [(0, 1), (1, 0), (2, 3), (3, 2)])

    near_back = lax.all_to_all(
        products.reshape(8, 8, 2, rows, width), ("xh", "xl", "yl"), 0, 0, tiled=True
    )
    near_sum = pl.pallas_call(
        sum_kernel,
        out_shape=shape(8, 2, rows, width),
        in_specs=[VMEM],
        out_specs=VMEM,
        compiler_params=PARAMS,
        name="near_sum",
    )(near_back)
    chosen = pl.pallas_call(
        choose_kernel,
        out_shape=shape(blocks, 2, rows, width),
        in_specs=[SMEM, SMEM, VMEM, VMEM],
        out_specs=VMEM,
        compiler_params=PARAMS,
        name="choose",
    )(place, partner, chip, next_chip)
    from_far = lax.ppermute(chosen, "zh", [(0, 2), (2, 0), (1, 3), (3, 1)])
    near_sum, from_far = lax.optimization_barrier((near_sum, from_far))
    far_back = lax.all_to_all(near_sum, ("zl", "yh"), 0, 0, tiled=True)

    shifted = pl.pallas_call(
        shift_kernel,
        out_shape=shape(blocks, 2, rows, width),
        in_specs=[SMEM, SMEM] + [VMEM] * 4,
        out_specs=VMEM,
        compiler_params=PARAMS,
        cost_estimate=pl.CostEstimate(
            flops=3 * 2 * 32 * 512**2, bytes_accessed=3 * 2**20, transcendentals=0
        ),
        name="shift",
    )(place, partner, chip, next_chip, from_far, shift_ops)

    return pl.pallas_call(
        final_kernel,
        out_shape=(shape(blocks, rows, width), shape(blocks, rows, width)),
        in_specs=[SMEM, SMEM, VMEM, VMEM],
        out_specs=(VMEM, VMEM),
        compiler_params=PARAMS,
        name="finish",
    )(place, block_dims, far_back, shifted)


def solution(mesh):
    fine = Mesh(mesh.devices.reshape(SIZES), AXES)
    in_specs = (
        P(WF, OPS, None),
        P(WF, OPS, None),
        P(OPS, WF, None, None),
        P(OPS, WF, None, None),
        P(WF, None, None),
        P(),
        P(),
    )
    out_specs = (P(WF, OPS, None), P(WF, OPS, None))
    return jax.shard_map(
        per_device, mesh=fine, in_specs=in_specs, out_specs=out_specs, check_vma=False
    )
```

```python
import functools

import jax
import jax.numpy as jnp
import numpy as np
from jax import lax
from jax.experimental import pallas as pl
from jax.experimental.pallas import tpu as pltpu
from jax.sharding import Mesh, PartitionSpec as P

AXES = ("xh", "xl", "zl", "yh", "yl", "zh", "c")
SIZES = (2, 2, 2, 4, 2, 4, 2)
OPS = ("xh", "xl", "zl", "yh", "yl")
WF = ("zh", "c")
F32 = jnp.float32
BF16 = jnp.bfloat16
VMEM = pl.BlockSpec(memory_space=pltpu.VMEM)
SMEM = pl.BlockSpec(memory_space=pltpu.SMEM)
HBM = pl.BlockSpec(memory_space=pl.ANY)
PARAMS = pltpu.CompilerParams(vmem_limit_bytes=48 * 1024 * 1024)
OWN = pltpu.CompilerParams(vmem_limit_bytes=46 * 1024 * 1024)
MAIN = pltpu.CompilerParams(vmem_limit_bytes=48 * 1024 * 1024)
WIDE = pltpu.CompilerParams(vmem_limit_bytes=60 * 1024 * 1024)


def far_groups():
    device = np.arange(512).reshape(4, 2, 4, 2, 4, 2)
    groups = []
    for parity in range(2):
        lines = np.stack([device[:, 0, :, parity], device[:, 1, :, 1 - parity]])
        groups.extend(lines.transpose(1, 3, 4, 0, 2).reshape(-1, 8).tolist())
    return groups


def shape(*dims):
    return jax.ShapeDtypeStruct(dims, F32)


def halves(value):
    high = value.astype(BF16)
    return high, (value - high.astype(F32)).astype(BF16)


def times(a, b):
    return jnp.dot(a, b, preferred_element_type=F32)


def times_t(a, b):
    return lax.dot_general(a, b, (((1,), (1,)), ((), ())), preferred_element_type=F32)


def live_mask(place_ref, dims_ref, block, rows, width):
    size = dims_ref[place_ref[1] * 2 + block]
    row = place_ref[0] * rows + lax.broadcasted_iota(jnp.int32, (rows, width), 0)
    column = lax.broadcasted_iota(jnp.int32, (rows, width), 1)
    return (row < size) & (column < size)


def swap(value):
    return lax.ppermute(value, "zl", [(0, 1), (1, 0)])


def after(value, earlier):
    return lax.optimization_barrier((value, earlier))[0]


def pick_kernel(spot_ref, left_ref, right_ref, out_ref, held, in_sems, out_sems):
    quarter = held.shape[1] // 4
    pieces = [(side, pl.ds(i * quarter, quarter)) for side in range(2) for i in range(4)]
    ins, outs = [], []
    for at, (side, rows) in enumerate(pieces):
        source = (left_ref, right_ref)[side].at[0, 1 - spot_ref[0], rows]
        ins.append(pltpu.make_async_copy(source, held.at[side, rows], in_sems.at[at]))
        outs.append(
            pltpu.make_async_copy(held.at[side, rows], out_ref.at[side, rows], out_sems.at[at])
        )
    for copy in ins:
        copy.start()
    for copy_in, copy_out in zip(ins, outs):
        copy_in.wait()
        copy_out.start()
    for copy in outs:
        copy.wait()


def spread_kernel(place_ref, dims_ref, one_ref, two_ref, far_ref, live_ref):
    blocks, rows, width = one_ref.shape
    for block in range(blocks):
        mask = live_mask(place_ref, dims_ref, block, rows, width)
        for vector, ref in enumerate((one_ref, two_ref)):
            live = jnp.where(mask, ref[block], 0.0)
            live_ref[block, vector] = live
            for slot in range(4):
                far_ref[block * 4 + slot, vector] = live


def own_kernel(place_ref, g_ref, l_ref, ph, pw, mh, ml, g, left, sems):
    width = g.shape[-1]
    half = width // 2
    mine = place_ref[0] // 8 % 2
    loads = [
        pltpu.make_async_copy(g_ref, g, sems.at[0]),
        pltpu.make_async_copy(l_ref.at[0, mine], left, sems.at[1]),
    ]
    for load in loads:
        load.start()
    loads[0].wait()
    for v in range(2):
        for x in range(4):
            for z in range(2):
                parts = [g[x, (yl + z + mine) % 2, z, :, v] for yl in range(2)]
                part = jnp.stack(parts, axis=1).reshape(64, width)
                rows = pl.ds(x * 128 + z * 64, 64)
                ph[v, rows], pw[v, rows] = halves(part)
    loads[1].wait()
    for i in range(2):
        rows = pl.ds(i * half, half)
        high, low = halves(left[rows])
        for v in range(2):
            m = times(high, ph[v]) + times(low, ph[v]) + times(high, pw[v])
            mh[v, rows], ml[v, rows] = halves(m)


def product_kernel(
    place_ref, ph, pw, own_h, own_l, r_ref, pair_ref, out_ref,
    ops, out, mh, ml, rh, rl, sems, out_sems,
):
    width = ops.shape[-1]
    half = width // 2
    mine = place_ref[0] // 8 % 2
    sources = (pair_ref.at[0], r_ref.at[0, mine], pair_ref.at[1])
    loads = [
        pltpu.make_async_copy(source, ops.at[at], sems.at[at]) for at, source in enumerate(sources)
    ]
    for load in loads:
        load.start()
    loads[0].wait()
    for i in range(2):
        rows = pl.ds(i * half, half)
        high, low = halves(ops[0, rows])
        for v in range(2):
            m = times(high, ph[v]) + times(low, ph[v]) + times(high, pw[v])
            mh[v, rows], ml[v, rows] = halves(m)
    for t in range(2):
        loads[1 + t].wait()
        rh[t], rl[t] = halves(ops[1 + t])
    stores = []
    for v in range(2):
        for i in range(2):
            rows = pl.ds(i * half, half)
            s = times_t(own_h[v, rows], rh[0]) + times_t(own_l[v, rows], rh[0])
            s += times_t(own_h[v, rows], rl[0]) + times_t(mh[v, rows], rh[1])
            s += times_t(ml[v, rows], rh[1]) + times_t(mh[v, rows], rl[1])
            s = s.reshape(2, 2, 4, 2, 8, width)
            for xl in range(2):
                for yl in range(2):
                    out[i, xl, yl, :, :, v] = s[xl, :, :, yl]
            place = (i, slice(None), slice(None), slice(None), slice(None), v)
            stores.append(
                pltpu.make_async_copy(out.at[place], out_ref.at[place], out_sems.at[v * 2 + i])
            )
            stores[-1].start()
    for store in stores:
        store.wait()


def sum_kernel(in_ref, out_ref):
    total = in_ref[0]
    for source in range(1, in_ref.shape[0]):
        total = total + in_ref[source]
    out_ref[...] = total


def held_rows(place_ref, pair, chip_ref, next_ref):
    wf, core = place_ref[1], (pair // 2 + place_ref[1]) % 2
    here = (pair // 4 + wf // 2) % 2 == 0
    return jnp.where(here, chip_ref[core, pair % 2], next_ref[core, pair % 2])


def choose_kernel(place_ref, pair_ref, chip_ref, next_ref, out_ref):
    far_wf = (place_ref[1] + 4) % 8
    for block in range(out_ref.shape[0]):
        out_ref[block] = held_rows(place_ref, pair_ref[far_wf * 2 + block], chip_ref, next_ref)


def shift_kernel(place_ref, pair_ref, chip_ref, next_ref, far_ref, shift_ref, out_ref):
    blocks, width = shift_ref.shape[0], shift_ref.shape[-1]
    for block in range(blocks):
        pair = pair_ref[place_ref[1] * 2 + block]
        held = pair // 8 == place_ref[1] // 4
        paired = jnp.where(held, held_rows(place_ref, pair, chip_ref, next_ref), far_ref[block])
        high, low = halves(paired.reshape(16, width))
        s_high, s_low = halves(shift_ref[block])
        out = times_t(high, s_high) + times_t(low, s_high) + times_t(high, s_low)
        out_ref[block] = out.reshape(2, 8, width)


def final_kernel(place_ref, dims_ref, back_ref, shifted_ref, one_ref, two_ref):
    blocks, rows, width = one_ref.shape
    for block in range(blocks):
        mask = live_mask(place_ref, dims_ref, block, rows, width)
        for vector, ref in enumerate((one_ref, two_ref)):
            total = shifted_ref[block, vector]
            for source in range(4):
                total = total + back_ref[block * 4 + source, vector]
            ref[block] = jnp.where(mask, total, 0.0)


def per_device(psi_one, psi_two, left_ops, right_ops, shift_ops, block_dims, partner):
    blocks, rows, width = psi_one.shape
    place = jnp.stack([lax.axis_index(OPS), lax.axis_index(WF)]).astype(jnp.int32)

    mine = lax.axis_index("zl").astype(jnp.int32)
    spot = mine[None]
    pair_out = pl.pallas_call(
        pick_kernel,
        out_shape=shape(2, width, width),
        in_specs=[SMEM, HBM, HBM],
        out_specs=HBM,
        scratch_shapes=[
            pltpu.VMEM((2, width, width), F32),
            pltpu.SemaphoreType.DMA((8,)),
            pltpu.SemaphoreType.DMA((8,)),
        ],
        compiler_params=WIDE,
        name="pick",
    )(spot, left_ops, right_ops)
    pair_in = swap(pair_out)

    far_out, live = pl.pallas_call(
        spread_kernel,
        out_shape=(shape(8, 2, rows, width), shape(blocks, 2, rows, width)),
        in_specs=[SMEM, SMEM, VMEM, VMEM],
        out_specs=(VMEM, VMEM),
        compiler_params=PARAMS,
        name="spread",
    )(place, block_dims, psi_one, psi_two)
    far_in = lax.all_to_all(
        far_out, AXES, 0, 0, tiled=True, axis_index_groups=far_groups()
    )

    other_core = lax.ppermute(live, "c", [(0, 1), (1, 0)])
    far_in, other_core = lax.optimization_barrier((far_in, other_core))

    near_in = lax.cond(
        lax.optimization_barrier(jnp.bool_(True)),
        lambda value: lax.all_to_all(
            jnp.broadcast_to(value[None], (8,) + value.shape), ("xh", "xl", "yl"), 0, 0, tiled=True
        ),
        lambda value: jnp.zeros((8,) + value.shape, F32),
        far_in,
    )
    near_in = lax.optimization_barrier(near_in)
    half_array = jax.ShapeDtypeStruct((2, width, width), BF16)
    own = pl.pallas_call(
        own_kernel,
        out_shape=(half_array,) * 4,
        in_specs=[SMEM, HBM, HBM],
        out_specs=(VMEM,) * 4,
        scratch_shapes=[
            pltpu.VMEM((4, 2, 2, 4, 2, rows, width), F32),
            pltpu.VMEM((width, width), F32),
            pltpu.SemaphoreType.DMA((2,)),
        ],
        compiler_params=OWN,
        cost_estimate=pl.CostEstimate(
            flops=6 * 2 * 512**3, bytes_accessed=7 * 2**20, transcendentals=0
        ),
        name="own",
    )(place, near_in.reshape(4, 2, 2, 4, 2, rows, width), left_ops)

    products = pl.pallas_call(
        product_kernel,
        out_shape=shape(2, 2, 2, 2, 4, 2, rows, width),
        in_specs=[SMEM, VMEM, VMEM, VMEM, VMEM, HBM, HBM],
        out_specs=HBM,
        scratch_shapes=[
            pltpu.VMEM((3, width, width), F32),
            pltpu.VMEM((2, 2, 2, 2, 4, 2, rows, width), F32),
            pltpu.VMEM((2, width, width), BF16),
            pltpu.VMEM((2, width, width), BF16),
            pltpu.VMEM((2, width, width), BF16),
            pltpu.VMEM((2, width, width), BF16),
            pltpu.SemaphoreType.DMA((3,)),
            pltpu.SemaphoreType.DMA((4,)),
        ],
        compiler_params=MAIN,
        cost_estimate=pl.CostEstimate(
            flops=18 * 2 * 512**3, bytes_accessed=9 * 2**20, transcendentals=0
        ),
        name="products",
    )(place, *own, right_ops, pair_in)

    chip = after(jnp.stack([live, other_core]), near_in)
    next_chip = lax.ppermute(chip, "zh", [(0, 1), (1, 0), (2, 3), (3, 2)])

    near_back = lax.all_to_all(
        products.reshape(8, 8, 2, rows, width), ("xh", "xl", "yl"), 0, 0, tiled=True
    )
    near_sum = pl.pallas_call(
        sum_kernel,
        out_shape=shape(8, 2, rows, width),
        in_specs=[VMEM],
        out_specs=VMEM,
        compiler_params=PARAMS,
        name="near_sum",
    )(near_back)
    chosen = pl.pallas_call(
        choose_kernel,
        out_shape=shape(blocks, 2, rows, width),
        in_specs=[SMEM, SMEM, VMEM, VMEM],
        out_specs=VMEM,
        compiler_params=PARAMS,
        name="choose",
    )(place, partner, chip, next_chip)
    from_far = lax.ppermute(chosen, "zh", [(0, 2), (2, 0), (1, 3), (3, 1)])
    near_sum, from_far = lax.optimization_barrier((near_sum, from_far))
    far_back = lax.all_to_all(near_sum, ("zl", "yh"), 0, 0, tiled=True)

    shifted = pl.pallas_call(
        shift_kernel,
        out_shape=shape(blocks, 2, rows, width),
        in_specs=[SMEM, SMEM] + [VMEM] * 4,
        out_specs=VMEM,
        compiler_params=PARAMS,
        cost_estimate=pl.CostEstimate(
            flops=3 * 2 * 32 * 512**2, bytes_accessed=3 * 2**20, transcendentals=0
        ),
        name="shift",
    )(place, partner, chip, next_chip, from_far, shift_ops)

    return pl.pallas_call(
        final_kernel,
        out_shape=(shape(blocks, rows, width), shape(blocks, rows, width)),
        in_specs=[SMEM, SMEM, VMEM, VMEM],
        out_specs=(VMEM, VMEM),
        compiler_params=PARAMS,
        name="finish",
    )(place, block_dims, far_back, shifted)


def solution(mesh):
    fine = Mesh(mesh.devices.reshape(SIZES), AXES)
    in_specs = (
        P(WF, OPS, None),
        P(WF, OPS, None),
        P(OPS, WF, None, None),
        P(OPS, WF, None, None),
        P(WF, None, None),
        P(),
        P(),
    )
    out_specs = (P(WF, OPS, None), P(WF, OPS, None))
    return jax.shard_map(
        per_device, mesh=fine, in_specs=in_specs, out_specs=out_specs, check_vma=False
    )
```

```python
import functools

import jax
import jax.numpy as jnp
import numpy as np
from jax import lax
from jax.experimental import pallas as pl
from jax.experimental.pallas import tpu as pltpu
from jax.sharding import Mesh, PartitionSpec as P

AXES = ("xh", "xl", "zl", "yh", "yl", "zh", "c")
SIZES = (2, 2, 2, 4, 2, 4, 2)
OPS = ("xh", "xl", "zl", "yh", "yl")
WF = ("zh", "c")
F32 = jnp.float32
BF16 = jnp.bfloat16
VMEM = pl.BlockSpec(memory_space=pltpu.VMEM)
SMEM = pl.BlockSpec(memory_space=pltpu.SMEM)
HBM = pl.BlockSpec(memory_space=pl.ANY)
PARAMS = pltpu.CompilerParams(vmem_limit_bytes=48 * 1024 * 1024)
OWN = pltpu.CompilerParams(vmem_limit_bytes=46 * 1024 * 1024)
MAIN = pltpu.CompilerParams(vmem_limit_bytes=47 * 1024 * 1024)
WIDE = pltpu.CompilerParams(vmem_limit_bytes=60 * 1024 * 1024)


def far_groups():
    device = np.arange(512).reshape(4, 2, 4, 2, 4, 2)
    groups = []
    for parity in range(2):
        lines = np.stack([device[:, 0, :, parity], device[:, 1, :, 1 - parity]])
        groups.extend(lines.transpose(1, 3, 4, 0, 2).reshape(-1, 8).tolist())
    return groups


def shape(*dims):
    return jax.ShapeDtypeStruct(dims, F32)


def halves(value):
    high = value.astype(BF16)
    return high, (value - high.astype(F32)).astype(BF16)


def times(a, b):
    return jnp.dot(a, b, preferred_element_type=F32)


def times_t(a, b):
    return lax.dot_general(a, b, (((1,), (1,)), ((), ())), preferred_element_type=F32)


def live_mask(place_ref, dims_ref, block, rows, width):
    size = dims_ref[place_ref[1] * 2 + block]
    row = place_ref[0] * rows + lax.broadcasted_iota(jnp.int32, (rows, width), 0)
    column = lax.broadcasted_iota(jnp.int32, (rows, width), 1)
    return (row < size) & (column < size)


def swap(value):
    return lax.ppermute(value, "zl", [(0, 1), (1, 0)])


def after(value, earlier):
    return lax.optimization_barrier((value, earlier))[0]


def pick_kernel(spot_ref, left_ref, right_ref, out_ref, held, in_sems, out_sems):
    quarter = held.shape[1] // 4
    pieces = [(side, pl.ds(i * quarter, quarter)) for side in range(2) for i in range(4)]
    ins, outs = [], []
    for at, (side, rows) in enumerate(pieces):
        source = (left_ref, right_ref)[side].at[0, 1 - spot_ref[0], rows]
        ins.append(pltpu.make_async_copy(source, held.at[side, rows], in_sems.at[at]))
        outs.append(
            pltpu.make_async_copy(held.at[side, rows], out_ref.at[side, rows], out_sems.at[at])
        )
    for copy in ins:
        copy.start()
    for copy_in, copy_out in zip(ins, outs):
        copy_in.wait()
        copy_out.start()
    for copy in outs:
        copy.wait()


def spread_kernel(place_ref, dims_ref, one_ref, two_ref, far_ref, live_ref):
    blocks, rows, width = one_ref.shape
    for block in range(blocks):
        mask = live_mask(place_ref, dims_ref, block, rows, width)
        for vector, ref in enumerate((one_ref, two_ref)):
            live = jnp.where(mask, ref[block], 0.0)
            live_ref[block, vector] = live
            for slot in range(4):
                far_ref[block * 4 + slot, vector] = live


def own_kernel(place_ref, g_ref, l_ref, r_ref, ph, pw, mh, ml, rh, rl, g, left, right, sems):
    width = g.shape[-1]
    half = width // 2
    mine = place_ref[0] // 8 % 2
    loads = [
        pltpu.make_async_copy(g_ref, g, sems.at[0]),
        pltpu.make_async_copy(l_ref.at[0, mine], left, sems.at[1]),
        pltpu.make_async_copy(r_ref.at[0, mine], right, sems.at[2]),
    ]
    for load in loads:
        load.start()
    loads[0].wait()
    for v in range(2):
        for x in range(4):
            for z in range(2):
                parts = [g[x, (yl + z + mine) % 2, z, :, v] for yl in range(2)]
                part = jnp.stack(parts, axis=1).reshape(64, width)
                rows = pl.ds(x * 128 + z * 64, 64)
                ph[v, rows], pw[v, rows] = halves(part)
    loads[1].wait()
    for i in range(2):
        rows = pl.ds(i * half, half)
        high, low = halves(left[rows])
        for v in range(2):
            m = times(high, ph[v]) + times(low, ph[v]) + times(high, pw[v])
            mh[v, rows], ml[v, rows] = halves(m)
    loads[2].wait()
    rh[...], rl[...] = halves(right[...])


def product_kernel(
    place_ref, ph, pw, own_h, own_l, own_rh, own_rl, pair_ref, out_ref,
    ops, out, mh, ml, rh, rl, sems, out_sems,
):
    width = ops.shape[-1]
    half = width // 2
    sources = (pair_ref.at[0], pair_ref.at[1])
    loads = [
        pltpu.make_async_copy(source, ops.at[at], sems.at[at]) for at, source in enumerate(sources)
    ]
    for load in loads:
        load.start()
    loads[0].wait()
    for i in range(2):
        rows = pl.ds(i * half, half)
        high, low = halves(ops[0, rows])
        for v in range(2):
            m = times(high, ph[v]) + times(low, ph[v]) + times(high, pw[v])
            mh[v, rows], ml[v, rows] = halves(m)
    loads[1].wait()
    rh[...], rl[...] = halves(ops[1])
    stores = []
    for v in range(2):
        for i in range(2):
            rows = pl.ds(i * half, half)
            s = times_t(own_h[v, rows], own_rh[...]) + times_t(own_l[v, rows], own_rh[...])
            s += times_t(own_h[v, rows], own_rl[...]) + times_t(mh[v, rows], rh[...])
            s += times_t(ml[v, rows], rh[...]) + times_t(mh[v, rows], rl[...])
            s = s.reshape(2, 2, 4, 2, 8, width)
            for xl in range(2):
                for yl in range(2):
                    out[i, xl, yl, :, :, v] = s[xl, :, :, yl]
            place = (i, slice(None), slice(None), slice(None), slice(None), v)
            stores.append(
                pltpu.make_async_copy(out.at[place], out_ref.at[place], out_sems.at[v * 2 + i])
            )
            stores[-1].start()
    for store in stores:
        store.wait()


def sum_kernel(in_ref, out_ref):
    total = in_ref[0]
    for source in range(1, in_ref.shape[0]):
        total = total + in_ref[source]
    out_ref[...] = total


def held_rows(place_ref, pair, chip_ref, next_ref):
    wf, core = place_ref[1], (pair // 2 + place_ref[1]) % 2
    here = (pair // 4 + wf // 2) % 2 == 0
    return jnp.where(here, chip_ref[core, pair % 2], next_ref[core, pair % 2])


def choose_kernel(place_ref, pair_ref, chip_ref, next_ref, out_ref):
    far_wf = (place_ref[1] + 4) % 8
    for block in range(out_ref.shape[0]):
        out_ref[block] = held_rows(place_ref, pair_ref[far_wf * 2 + block], chip_ref, next_ref)


def shift_kernel(place_ref, pair_ref, chip_ref, next_ref, far_ref, shift_ref, out_ref):
    blocks, width = shift_ref.shape[0], shift_ref.shape[-1]
    for block in range(blocks):
        pair = pair_ref[place_ref[1] * 2 + block]
        held = pair // 8 == place_ref[1] // 4
        paired = jnp.where(held, held_rows(place_ref, pair, chip_ref, next_ref), far_ref[block])
        high, low = halves(paired.reshape(16, width))
        s_high, s_low = halves(shift_ref[block])
        out = times_t(high, s_high) + times_t(low, s_high) + times_t(high, s_low)
        out_ref[block] = out.reshape(2, 8, width)


def final_kernel(place_ref, dims_ref, back_ref, shifted_ref, one_ref, two_ref):
    blocks, rows, width = one_ref.shape
    for block in range(blocks):
        mask = live_mask(place_ref, dims_ref, block, rows, width)
        for vector, ref in enumerate((one_ref, two_ref)):
            total = shifted_ref[block, vector]
            for source in range(4):
                total = total + back_ref[block * 4 + source, vector]
            ref[block] = jnp.where(mask, total, 0.0)


def per_device(psi_one, psi_two, left_ops, right_ops, shift_ops, block_dims, partner):
    blocks, rows, width = psi_one.shape
    place = jnp.stack([lax.axis_index(OPS), lax.axis_index(WF)]).astype(jnp.int32)

    mine = lax.axis_index("zl").astype(jnp.int32)
    spot = mine[None]
    pair_out = pl.pallas_call(
        pick_kernel,
        out_shape=shape(2, width, width),
        in_specs=[SMEM, HBM, HBM],
        out_specs=HBM,
        scratch_shapes=[
            pltpu.VMEM((2, width, width), F32),
            pltpu.SemaphoreType.DMA((8,)),
            pltpu.SemaphoreType.DMA((8,)),
        ],
        compiler_params=WIDE,
        name="pick",
    )(spot, left_ops, right_ops)
    pair_in = swap(pair_out)

    far_out, live = pl.pallas_call(
        spread_kernel,
        out_shape=(shape(8, 2, rows, width), shape(blocks, 2, rows, width)),
        in_specs=[SMEM, SMEM, VMEM, VMEM],
        out_specs=(VMEM, VMEM),
        compiler_params=PARAMS,
        name="spread",
    )(place, block_dims, psi_one, psi_two)
    far_in = lax.all_to_all(
        far_out, AXES, 0, 0, tiled=True, axis_index_groups=far_groups()
    )

    other_core = lax.ppermute(live, "c", [(0, 1), (1, 0)])
    far_in, other_core = lax.optimization_barrier((far_in, other_core))

    near_in = lax.cond(
        lax.optimization_barrier(jnp.bool_(True)),
        lambda value: lax.all_to_all(
            jnp.broadcast_to(value[None], (8,) + value.shape), ("xh", "xl", "yl"), 0, 0, tiled=True
        ),
        lambda value: jnp.zeros((8,) + value.shape, F32),
        far_in,
    )
    near_in = lax.optimization_barrier(near_in)
    half_array = jax.ShapeDtypeStruct((2, width, width), BF16)
    own = pl.pallas_call(
        own_kernel,
        out_shape=(half_array,) * 4 + (jax.ShapeDtypeStruct((width, width), BF16),) * 2,
        in_specs=[SMEM, HBM, HBM, HBM],
        out_specs=(VMEM,) * 6,
        scratch_shapes=[
            pltpu.VMEM((4, 2, 2, 4, 2, rows, width), F32),
            pltpu.VMEM((width, width), F32),
            pltpu.VMEM((width, width), F32),
            pltpu.SemaphoreType.DMA((3,)),
        ],
        compiler_params=OWN,
        cost_estimate=pl.CostEstimate(
            flops=6 * 2 * 512**3, bytes_accessed=7 * 2**20, transcendentals=0
        ),
        name="own",
    )(place, near_in.reshape(4, 2, 2, 4, 2, rows, width), left_ops, right_ops)

    products = pl.pallas_call(
        product_kernel,
        out_shape=shape(2, 2, 2, 2, 4, 2, rows, width),
        in_specs=[SMEM] + [VMEM] * 6 + [HBM],
        out_specs=HBM,
        scratch_shapes=[
            pltpu.VMEM((2, width, width), F32),
            pltpu.VMEM((2, 2, 2, 2, 4, 2, rows, width), F32),
            pltpu.VMEM((2, width, width), BF16),
            pltpu.VMEM((2, width, width), BF16),
            pltpu.VMEM((width, width), BF16),
            pltpu.VMEM((width, width), BF16),
            pltpu.SemaphoreType.DMA((2,)),
            pltpu.SemaphoreType.DMA((4,)),
        ],
        compiler_params=MAIN,
        cost_estimate=pl.CostEstimate(
            flops=18 * 2 * 512**3, bytes_accessed=9 * 2**20, transcendentals=0
        ),
        name="products",
    )(place, *own, pair_in)

    chip = after(jnp.stack([live, other_core]), near_in)
    next_chip = lax.ppermute(chip, "zh", [(0, 1), (1, 0), (2, 3), (3, 2)])

    near_back = lax.all_to_all(
        products.reshape(8, 8, 2, rows, width), ("xh", "xl", "yl"), 0, 0, tiled=True
    )
    near_sum = pl.pallas_call(
        sum_kernel,
        out_shape=shape(8, 2, rows, width),
        in_specs=[VMEM],
        out_specs=VMEM,
        compiler_params=PARAMS,
        name="near_sum",
    )(near_back)
    chosen = pl.pallas_call(
        choose_kernel,
        out_shape=shape(blocks, 2, rows, width),
        in_specs=[SMEM, SMEM, VMEM, VMEM],
        out_specs=VMEM,
        compiler_params=PARAMS,
        name="choose",
    )(place, partner, chip, next_chip)
    from_far = lax.ppermute(chosen, "zh", [(0, 2), (2, 0), (1, 3), (3, 1)])
    near_sum, from_far = lax.optimization_barrier((near_sum, from_far))
    far_back = lax.all_to_all(near_sum, ("zl", "yh"), 0, 0, tiled=True)

    shifted = pl.pallas_call(
        shift_kernel,
        out_shape=shape(blocks, 2, rows, width),
        in_specs=[SMEM, SMEM] + [VMEM] * 4,
        out_specs=VMEM,
        compiler_params=PARAMS,
        cost_estimate=pl.CostEstimate(
            flops=3 * 2 * 32 * 512**2, bytes_accessed=3 * 2**20, transcendentals=0
        ),
        name="shift",
    )(place, partner, chip, next_chip, from_far, shift_ops)

    return pl.pallas_call(
        final_kernel,
        out_shape=(shape(blocks, rows, width), shape(blocks, rows, width)),
        in_specs=[SMEM, SMEM, VMEM, VMEM],
        out_specs=(VMEM, VMEM),
        compiler_params=PARAMS,
        name="finish",
    )(place, block_dims, far_back, shifted)


def solution(mesh):
    fine = Mesh(mesh.devices.reshape(SIZES), AXES)
    in_specs = (
        P(WF, OPS, None),
        P(WF, OPS, None),
        P(OPS, WF, None, None),
        P(OPS, WF, None, None),
        P(WF, None, None),
        P(),
        P(),
    )
    out_specs = (P(WF, OPS, None), P(WF, OPS, None))
    return jax.shard_map(
        per_device, mesh=fine, in_specs=in_specs, out_specs=out_specs, check_vma=False
    )
```
